32 devices in a mesh: ctx: 4 (over z), fsdp: 8 (over y, x, core).
Axes of the slice: x: 2, y: 2, z: 4, core: 2. Of those that a mesh axis runs over, the one named last changes fastest.
Arguments:
- clean: bfloat16 [1024, 5120], P(('ctx', 'fsdp')), may hold values from -6 to 6
- noise: bfloat16 [1024, 5120], P(('ctx', 'fsdp')), may hold values from -6 to 6
- noise_two: bfloat16 [1024, 5120], P(('ctx', 'fsdp')), may hold values from -6 to 6
- steps_gen: int32 [3], replicated, may hold values from 600 to 959
- steps_teacher: int32 [3], replicated, may hold values from 20 to 979
- cache_key: bfloat16 [1024, 4096], P('ctx', 'fsdp'), may hold values from -6 to 6
- cache_value: bfloat16 [1024, 4096], P('ctx', 'fsdp'), may hold values from -6 to 6
- cache_block: int32 [1024], P('ctx'), may hold values from 0 to 6
- span_block: int32 [1], replicated, may hold values from 2 to 6
- gen_query: bfloat16 [5120, 4096], P(None, 'fsdp'), may hold values from -0.07614237 to 0.07614237
- gen_key: bfloat16 [5120, 4096], P(None, 'fsdp'), may hold values from -0.052146567 to 0.052146567
- gen_value: bfloat16 [5120, 4096], P(None, 'fsdp'), may hold values from -0.078125 to 0.078125
- gen_out: bfloat16 [4096, 5120], P('fsdp'), may hold values from -0.375 to 0.375
- teacher_query: bfloat16 [5120, 4096], P(None, 'fsdp'), may hold values from -0.07614237 to 0.07614237
- teacher_key: bfloat16 [5120, 4096], P(None, 'fsdp'), may hold values from -0.052146567 to 0.052146567
- teacher_value: bfloat16 [5120, 4096], P(None, 'fsdp'), may hold values from -0.078125 to 0.078125
- teacher_out: bfloat16 [4096, 5120], P('fsdp'), may hold values from -0.375 to 0.375
Outputs:
- generated: bfloat16 [1024, 5120], P(('ctx', 'fsdp'))
- grad_out: bfloat16 [4096, 5120], P('fsdp')
The draws below stay inside these ranges and needn't reach their ends.
Inputs may be any that keep to these rules, and one draw needn't show every extreme that they name: span_block holds one id.
All inputs are finite; a program needn't handle non-finite values.
Results may differ from the reference program's by a relative error of at most 0.018.
The reference program's roundings to bfloat16 on the way count: a program that leaves them out, or rounds other values in their place, can miss the bound.
Values may be sent and summed in bfloat16 or wider, within the bound.
A program may use at most 128 MiB of HBM per device.

```python
import jax
import jax.numpy as jnp
from jax import lax

D = 5120
HEADS = 32
HEAD = 128
FRAMES = 3
STEPS = 1000
NBLK = 7
TOKENS = 1024
CACHE = 1024
INNER = 4096
N_FSDP = 8


def drawn_pair(key, query_scale):
    streams = jax.random.split(key, 5)
    query_base = jax.random.uniform(streams[0], (D, INNER), jnp.float32, -1.7, 1.7)
    key_base = jax.random.uniform(streams[1], (D, INNER), jnp.float32, -1.7, 1.7)
    feature_signs = jax.random.randint(streams[2], (D,), 0, 2).astype(jnp.float32) * 2.0 - 1.0
    head_signs = jax.random.randint(streams[3], (HEADS, HEAD), 0, 2).astype(jnp.float32) * 2.0 - 1.0
    shuffled = jax.random.permutation(streams[4], HEADS)
    aligned_count = max(HEADS // 8, 1)
    picked = (shuffled < aligned_count).astype(jnp.float32)
    amplitude = picked * 0.0
    direction = (amplitude[:, None] * head_signs / HEAD ** 0.5).reshape(INNER)
    outer_part = (feature_signs / D ** 0.5)[:, None] * direction[None, :]
    first = query_base * (query_scale / D ** 0.5) + outer_part
    second = key_base / D ** 0.5 + outer_part
    return (first, second)


def draw_gen_query(key, part):
    return drawn_pair(jax.random.fold_in(key, 11), 2.0)[0].astype(jnp.bfloat16)


def draw_gen_key(key, part):
    return drawn_pair(jax.random.fold_in(key, 11), 2.0)[1].astype(jnp.bfloat16)


def draw_teacher_query(key, part):
    return drawn_pair(jax.random.fold_in(key, 23), 2.0)[0].astype(jnp.bfloat16)


def draw_teacher_key(key, part):
    return drawn_pair(jax.random.fold_in(key, 23), 2.0)[1].astype(jnp.bfloat16)


def set_ends(drawn, rng, least, top_value):
    index_at = [jax.random.randint(jax.random.fold_in(rng, axis), (), 0, length) for axis, length in enumerate(drawn.shape)]
    longest = drawn.shape.index(max(drawn.shape))
    next_to = index_at[:longest] + [(index_at[longest] + 1) % drawn.shape[longest]] + index_at[longest + 1:]
    return drawn.at[tuple(index_at)].set(least).at[tuple(next_to)].set(top_value)


def levels(rng, shape, cuts, smallest, high):
    level = 1.0
    for axis_at, shards_of in cuts:
        draws = jax.random.uniform(jax.random.fold_in(jax.random.fold_in(rng, 6), axis_at), (shards_of,), jnp.float32, smallest / len(cuts), high / len(cuts))
        level = level * jnp.repeat(jnp.exp(draws), shape[axis_at] // shards_of).reshape((-1,) + (1,) * (len(shape) - 1 - axis_at))
    return level


def scatter_about(rng, shape, scale, limit, cuts=(), held_as=jnp.bfloat16):
    array = scale * jax.random.normal(rng, shape, jnp.float32)
    if cuts:
        array = array * levels(rng, shape, cuts, -0.22, 0.18)
    return jnp.clip(array, -limit, limit).astype(held_as)


def setup_inputs(seed: int = 0) -> dict:
    seeds = jax.random.split(jax.random.key(seed), 18)
    clean = scatter_about(seeds[0], (TOKENS, D), 1.0, 6.0, ((0, 32),))
    noise = scatter_about(seeds[1], (TOKENS, D), 1.0, 6.0, ((0, 32),))
    noise_two = scatter_about(seeds[2], (TOKENS, D), 1.0, 6.0, ((0, 32),))
    steps_gen = jax.random.randint(seeds[3], (FRAMES,), 600, 960).astype(jnp.int32)
    steps_teacher = jax.random.randint(seeds[4], (FRAMES,), 20, 980).astype(jnp.int32)
    cache_key = scatter_about(seeds[5], (CACHE, INNER), 1.0, 6.0, ((0, 4), (1, 8)))
    cache_value = scatter_about(seeds[6], (CACHE, INNER), 1.0, 6.0, ((0, 4), (1, 8)))
    cache_block = set_ends(jax.random.randint(seeds[7], (CACHE,), 0, NBLK), jax.random.fold_in(seeds[7], 1), 0, NBLK - 1).astype(jnp.int32)
    span_block = jax.random.randint(seeds[8], (1,), 2, NBLK).astype(jnp.int32)
    gen_query = draw_gen_query(jax.random.fold_in(seeds[17], 71), 0)
    gen_key = draw_gen_key(jax.random.fold_in(seeds[17], 71), 0)
    gen_value = scatter_about(seeds[11], (D, INNER), D ** -0.5, 0.078125, ((1, 8),))
    gen_out = scatter_about(seeds[12], (INNER, D), (INNER // 16) ** -0.5, 0.375, ((0, 8),))
    teacher_query = draw_teacher_query(jax.random.fold_in(seeds[17], 71), 0)
    teacher_key = draw_teacher_key(jax.random.fold_in(seeds[17], 71), 0)
    teacher_value = scatter_about(seeds[15], (D, INNER), D ** -0.5, 0.078125, ((1, 8),))
    teacher_out = scatter_about(seeds[16], (INNER, D), (INNER // 16) ** -0.5, 0.375, ((0, 8),))
    return {"clean": clean, "noise": noise, "noise_two": noise_two, "steps_gen": steps_gen, "steps_teacher": steps_teacher, "cache_key": cache_key, "cache_value": cache_value, "cache_block": cache_block, "span_block": span_block, "gen_query": gen_query, "gen_key": gen_key, "gen_value": gen_value, "gen_out": gen_out, "teacher_query": teacher_query, "teacher_key": teacher_key, "teacher_value": teacher_value, "teacher_out": teacher_out}


SHIFT = 5.0
EPS = 1e-06

def sigmas(steps, offset, count, total):
    level = 1.0 - steps.astype(jnp.float32) / STEPS
    sig = SHIFT * level / (1.0 + (SHIFT - 1.0) * level)
    positions = offset + jnp.arange(count, dtype=jnp.int32)
    frame = positions * FRAMES // total
    match = (frame[:, None] == jnp.arange(FRAMES, dtype=jnp.int32)[None, :]).astype(jnp.float32)
    return lax.optimization_barrier(jnp.sum(match * sig[None, :], axis=1))[:, None]

def normed(values):
    wide = values.astype(jnp.float32)
    return (wide * lax.rsqrt(lax.optimization_barrier(jnp.mean(wide * wide, axis=1, keepdims=True)) + EPS)).astype(jnp.bfloat16)

def attend(query, keys, values, allowed):
    scale = 1.0 / HEAD ** 0.5

    def single(head):
        start = head * HEAD
        q_head = lax.dynamic_slice_in_dim(query, start, HEAD, 1)
        k_head = lax.dynamic_slice_in_dim(keys, start, HEAD, 1)
        v_head = lax.dynamic_slice_in_dim(values, start, HEAD, 1)
        scores = jnp.dot(q_head, k_head.T, preferred_element_type=jnp.float32) * scale
        scores = jnp.where(allowed[None, :], scores, -1e+30)
        top = lax.optimization_barrier(jnp.max(scores, axis=1, keepdims=True))
        weights = jnp.where(allowed[None, :], jnp.exp(scores - top), 0.0)
        total = lax.optimization_barrier(jnp.sum(weights, axis=1, keepdims=True))
        return jnp.dot(weights.astype(jnp.bfloat16), v_head, preferred_element_type=jnp.float32) / total
    outputs = lax.map(single, jnp.arange(HEADS, dtype=jnp.int32))
    rows = query.shape[0]
    return jnp.transpose(outputs, (1, 0, 2)).reshape(rows, HEADS * HEAD).astype(jnp.bfloat16)

def grouped(attn, weight):
    width = HEADS * HEAD // N_FSDP

    def add(total, group):
        rows = lax.dynamic_slice_in_dim(attn, group * width, width, 1)
        cols = lax.dynamic_slice_in_dim(weight, group * width, width, 0)
        part = jnp.dot(rows, cols, preferred_element_type=jnp.float32)
        part = lax.optimization_barrier(part.astype(jnp.bfloat16)).astype(jnp.float32)
        return (total + part, None)
    start = jnp.zeros((attn.shape[0], weight.shape[1]), jnp.float32)
    total, _ = lax.scan(add, start, jnp.arange(N_FSDP, dtype=jnp.int32))
    return total

def reference(clean, noise, noise_two, steps_gen, steps_teacher, cache_key, cache_value, cache_block, span_block, gen_query, gen_key, gen_value, gen_out, teacher_query, teacher_key, teacher_value, teacher_out):
    total = clean.shape[0]
    sig_gen = sigmas(steps_gen, 0, total, total)
    sig_teacher = sigmas(steps_teacher, 0, total, total)
    mixed = ((1.0 - sig_gen) * clean.astype(jnp.float32) + sig_gen * noise.astype(jnp.float32)).astype(jnp.bfloat16)
    inputs = normed(mixed)
    query = jnp.dot(inputs, gen_query, preferred_element_type=jnp.float32).astype(jnp.bfloat16)
    key = jnp.dot(inputs, gen_key, preferred_element_type=jnp.float32).astype(jnp.bfloat16)
    value = jnp.dot(inputs, gen_value, preferred_element_type=jnp.float32).astype(jnp.bfloat16)
    allowed = jnp.concatenate([cache_block < span_block[0], jnp.ones((total,), bool)])
    attn = attend(query, jnp.concatenate([cache_key, key], 0), jnp.concatenate([cache_value, value], 0), allowed)
    generated = (mixed.astype(jnp.float32) + grouped(attn, gen_out)).astype(jnp.bfloat16)
    noisy = ((1.0 - sig_teacher) * generated.astype(jnp.float32) + sig_teacher * noise_two.astype(jnp.float32)).astype(jnp.bfloat16)
    inputs_two = normed(noisy)
    t_query = jnp.dot(inputs_two, teacher_query, preferred_element_type=jnp.float32).astype(jnp.bfloat16)
    t_key = jnp.dot(inputs_two, teacher_key, preferred_element_type=jnp.float32).astype(jnp.bfloat16)
    t_value = jnp.dot(inputs_two, teacher_value, preferred_element_type=jnp.float32).astype(jnp.bfloat16)
    teacher_attn = attend(t_query, t_key, t_value, jnp.ones((total,), bool))
    real = noisy.astype(jnp.float32) + grouped(teacher_attn, teacher_out)
    cotangent = (generated.astype(jnp.float32) - real).astype(jnp.bfloat16)
    grad_out = jnp.dot(attn.T, cotangent, preferred_element_type=jnp.float32).astype(jnp.bfloat16)
    return (generated, grad_out)
```

```python
import jax
import jax.numpy as jnp
from jax import lax
from jax.sharding import PartitionSpec as P

HEAD = 128
FRAMES = 3
STEPS = 1000


SHIFT = 5.0
EPS = 1e-06


def sigmas(steps, offset, count, total):
    level = 1.0 - steps.astype(jnp.float32) / STEPS
    sig = SHIFT * level / (1.0 + (SHIFT - 1.0) * level)
    positions = offset + jnp.arange(count, dtype=jnp.int32)
    frame = positions * FRAMES // total
    match = (frame[:, None] == jnp.arange(FRAMES, dtype=jnp.int32)[None, :]).astype(jnp.float32)
    return jnp.sum(match * sig[None, :], axis=1)[:, None]


def normed(values):
    wide = values.astype(jnp.float32)
    return (wide * lax.rsqrt(jnp.mean(wide * wide, axis=1, keepdims=True) + EPS)).astype(
        jnp.bfloat16
    )


def attend(query_heads, parts):
    head_size = query_heads.shape[2]
    scale = 1.0 / head_size**0.5
    all_scores = []
    for keys, _, allowed in parts:
        scores = (
            jnp.einsum("rhd,phd->hrp", query_heads, keys, preferred_element_type=jnp.float32)
            * scale
        )
        if allowed is not None:
            scores = jnp.where(allowed[None, None, :], scores, -1e30)
        all_scores.append(scores)
    top = all_scores[0].max(axis=2)
    for scores in all_scores[1:]:
        top = jnp.maximum(top, scores.max(axis=2))
    total = 0.0
    accum = 0.0
    for scores, (_, values, allowed) in zip(all_scores, parts):
        weights = jnp.exp(scores - top[:, :, None])
        if allowed is not None:
            weights = jnp.where(allowed[None, None, :], weights, 0.0)
        total = total + weights.sum(axis=2)
        accum = accum + jnp.einsum(
            "hrp,phd->hrd",
            weights.astype(jnp.bfloat16),
            values,
            preferred_element_type=jnp.float32,
        )
    heads, rows, _ = accum.shape
    result = accum / total[:, :, None]
    return jnp.transpose(result, (1, 0, 2)).reshape(rows, heads * head_size).astype(jnp.bfloat16)


def per_device(
    clean,
    noise,
    noise_two,
    steps_gen,
    steps_teacher,
    cache_key,
    cache_value,
    cache_block,
    span_block,
    gen_query,
    gen_key,
    gen_value,
    gen_out,
    teacher_query,
    teacher_key,
    teacher_value,
    teacher_out,
):
    ctx_count = lax.axis_size("ctx")
    fsdp_count = lax.axis_size("fsdp")
    tok_dev = clean.shape[0]
    block_rows = tok_dev * fsdp_count
    total = block_rows * ctx_count
    offset = (lax.axis_index("ctx") * fsdp_count + lax.axis_index("fsdp")) * tok_dev
    width = gen_query.shape[1]
    heads = width // HEAD
    sig_gen = sigmas(steps_gen, offset, tok_dev, total)
    mixed = (
        (1.0 - sig_gen) * clean.astype(jnp.float32) + sig_gen * noise.astype(jnp.float32)
    ).astype(jnp.bfloat16)
    slots = cache_block.shape[0]
    visible = (cache_block < span_block[0]).astype(jnp.bfloat16)
    flag_rows = -(-slots // (16 * width)) * 16
    flags = jnp.pad(visible, (0, flag_rows * width - slots)).reshape(flag_rows, width)
    cache = lax.all_gather(
        jnp.concatenate([cache_key, cache_value, flags], axis=0), "ctx", axis=0, tiled=False
    )
    gen_stack = jnp.concatenate([gen_query, gen_key, gen_value], axis=1)
    projected = jnp.dot(
        normed(lax.all_gather(mixed, "fsdp", axis=0, tiled=True)),
        gen_stack,
        preferred_element_type=jnp.float32,
    ).astype(jnp.bfloat16)
    query_heads = projected[:, :width].reshape(block_rows, heads, HEAD)
    span = lax.all_gather(projected[:, width:], "ctx", axis=0, tiled=True)
    slots_all = slots * ctx_count
    cached_keys = cache[:, :slots].reshape(slots_all, heads, HEAD)
    cached_values = cache[:, slots : 2 * slots].reshape(slots_all, heads, HEAD)
    allowed = cache[:, 2 * slots :].reshape(ctx_count, -1)[:, :slots].reshape(-1) > 0
    attn = attend(
        query_heads,
        (
            (cached_keys, cached_values, allowed),
            (
                span[:, :width].reshape(total, heads, HEAD),
                span[:, width:].reshape(total, heads, HEAD),
                None,
            ),
        ),
    )
    attn_all = lax.all_gather(attn, "ctx", axis=0, tiled=True)
    gen_sum = lax.psum_scatter(
        jnp.dot(attn, gen_out, preferred_element_type=jnp.float32).astype(jnp.bfloat16),
        "fsdp",
        scatter_dimension=0,
        tiled=True,
    ).astype(jnp.float32)
    generated = (mixed.astype(jnp.float32) + gen_sum).astype(jnp.bfloat16)
    sig_teacher = sigmas(steps_teacher, offset, tok_dev, total)
    noisy = (
        (1.0 - sig_teacher) * generated.astype(jnp.float32)
        + sig_teacher * noise_two.astype(jnp.float32)
    ).astype(jnp.bfloat16)
    teacher_stack = jnp.concatenate([teacher_query, teacher_key, teacher_value], axis=1)
    teacher_proj = jnp.dot(
        normed(lax.all_gather(noisy, "fsdp", axis=0, tiled=True)),
        teacher_stack,
        preferred_element_type=jnp.float32,
    ).astype(jnp.bfloat16)
    teacher_heads = teacher_proj[:, :width].reshape(block_rows, heads, HEAD)
    t_span = lax.all_gather(teacher_proj[:, width:], "ctx", axis=0, tiled=True)
    teacher_attn = attend(
        teacher_heads,
        (
            (
                t_span[:, :width].reshape(total, heads, HEAD),
                t_span[:, width:].reshape(total, heads, HEAD),
                None,
            ),
        ),
    )
    teacher_sum = lax.psum_scatter(
        jnp.dot(teacher_attn, teacher_out, preferred_element_type=jnp.float32).astype(jnp.bfloat16),
        "fsdp",
        scatter_dimension=0,
        tiled=True,
    ).astype(jnp.float32)
    real = noisy.astype(jnp.float32) + teacher_sum
    cotangent = (generated.astype(jnp.float32) - real).astype(jnp.bfloat16)
    grad_out = lax.dot_general(
        attn_all,
        lax.all_gather(cotangent, ("ctx", "fsdp"), axis=0, tiled=True),
        (((0,), (0,)), ((), ())),
        preferred_element_type=jnp.float32,
    ).astype(jnp.bfloat16)
    return (generated, grad_out)


def solution(mesh):
    in_specs = (
        P(("ctx", "fsdp"), None),
        P(("ctx", "fsdp"), None),
        P(("ctx", "fsdp"), None),
        P(),
        P(),
        P("ctx", "fsdp"),
        P("ctx", "fsdp"),
        P("ctx"),
        P(),
        P(None, "fsdp"),
        P(None, "fsdp"),
        P(None, "fsdp"),
        P("fsdp", None),
        P(None, "fsdp"),
        P(None, "fsdp"),
        P(None, "fsdp"),
        P("fsdp", None),
    )
    out_specs = (P(("ctx", "fsdp"), None), P("fsdp", None))
    return jax.shard_map(
        per_device, mesh=mesh, in_specs=in_specs, out_specs=out_specs, check_vma=False
    )
```

```python
import functools

import jax
import jax.numpy as jnp
from jax import lax
from jax.experimental import pallas as pl
from jax.experimental.pallas import tpu as pltpu
from jax.sharding import PartitionSpec as P

HEAD = 128
FRAMES = 3
STEPS = 1000


SHIFT = 5.0
EPS = 1e-06


def sigmas(steps, offset, count, total):
    level = 1.0 - steps.astype(jnp.float32) / STEPS
    sig = SHIFT * level / (1.0 + (SHIFT - 1.0) * level)
    positions = offset + jnp.arange(count, dtype=jnp.int32)
    frame = positions * FRAMES // total
    match = (frame[:, None] == jnp.arange(FRAMES, dtype=jnp.int32)[None, :]).astype(jnp.float32)
    return jnp.sum(match * sig[None, :], axis=1)[:, None]


def normed(values):
    wide = values.astype(jnp.float32)
    return (wide * lax.rsqrt(jnp.mean(wide * wide, axis=1, keepdims=True) + EPS)).astype(
        jnp.bfloat16
    )


def attend(query_heads, parts):
    head_size = query_heads.shape[2]
    scale = 1.0 / head_size**0.5
    all_scores = []
    for keys, _, allowed in parts:
        scores = (
            jnp.einsum("rhd,phd->hrp", query_heads, keys, preferred_element_type=jnp.float32)
            * scale
        )
        if allowed is not None:
            scores = jnp.where(allowed[None, None, :], scores, -1e30)
        all_scores.append(scores)
    top = all_scores[0].max(axis=2)
    for scores in all_scores[1:]:
        top = jnp.maximum(top, scores.max(axis=2))
    total = 0.0
    accum = 0.0
    for scores, (_, values, allowed) in zip(all_scores, parts):
        weights = jnp.exp(scores - top[:, :, None])
        if allowed is not None:
            weights = jnp.where(allowed[None, None, :], weights, 0.0)
        total = total + weights.sum(axis=2)
        accum = accum + jnp.einsum(
            "hrp,phd->hrd",
            weights.astype(jnp.bfloat16),
            values,
            preferred_element_type=jnp.float32,
        )
    heads, rows, _ = accum.shape
    result = accum / total[:, :, None]
    return jnp.transpose(result, (1, 0, 2)).reshape(rows, heads * head_size).astype(jnp.bfloat16)


MESH = pl.DeviceIdType.MESH
VMEM_BYTES = 40 * 1024 * 1024


class Place:
    def __init__(self, ctx_count, fsdp_count):
        self.ctx_count = ctx_count
        self.count = fsdp_count
        self.chips = fsdp_count // 2
        self.z = lax.axis_index("ctx")
        self.me = lax.axis_index("fsdp")
        self.chip = lax.div(self.me, 2)
        self.core = lax.rem(self.me, 2)
        self.sibling = self.chip * 2 + 1 - self.core

    def ahead(self, step):
        return lax.rem(self.chip + step, self.chips) * 2

    def behind(self, step):
        return lax.rem(self.chip + self.chips - step, self.chips) * 2

    def group_targets(self):
        same_core = [(self.z, self.ahead(j) + self.core) for j in range(1, self.chips)]
        return same_core + [(self.z, self.sibling)]

    def ctx_ahead(self, step):
        return lax.rem(self.z + step, self.ctx_count)

    def ctx_behind(self, step):
        return lax.rem(self.z + self.ctx_count - step, self.ctx_count)

    def ctx_targets(self):
        return [(self.ctx_ahead(i), self.me) for i in range(1, self.ctx_count)]


def greet(targets):
    barrier = pltpu.get_barrier_semaphore()
    for target in targets:
        pl.semaphore_signal(barrier, inc=1, device_id=target, device_id_type=MESH)
    pl.semaphore_wait(barrier, len(targets))


def remote(src, dst, send_sem, recv_sem, target):
    return pltpu.make_async_remote_copy(
        src_ref=src,
        dst_ref=dst,
        send_sem=send_sem,
        recv_sem=recv_sem,
        device_id=target,
        device_id_type=MESH,
    )


class Spread:
    def __init__(self, place, src, out, row, sems, index):
        self.place, self.src, self.out, self.row = place, src, out, row
        self.send, self.recv, self.relay_send, self.relay_recv = (s.at[index] for s in sems)
        self.relays = []

    def own(self, step):
        p = self.place
        target = (p.z, p.sibling if step == 0 else p.ahead(step) + p.core)
        return remote(
            self.src, self.out.at[self.row + p.me], self.send.at[step], self.recv.at[step], target
        )

    def arrival(self, step):
        p = self.place
        source = p.sibling if step == 0 else p.behind(step) + p.core
        return remote(
            self.src,
            self.out.at[self.row + source],
            self.send.at[step],
            self.recv.at[step],
            (p.z, p.sibling),
        )

    def relay(self, step, core):
        p = self.place
        block = self.out.at[self.row + p.behind(step) + core]
        return remote(
            block, block, self.relay_send.at[step], self.relay_recv.at[step], (p.z, p.sibling)
        )

    def start(self):
        for step in list(range(1, self.place.chips)) + [0]:
            self.own(step).start()

    def forward(self):
        for step in range(1, self.place.chips):
            self.arrival(step).wait_recv()
            self.relay(step, self.place.core).start()

    def end(self):
        p = self.place
        self.arrival(0).wait_recv()
        for step in range(1, p.chips):
            self.relay(step, 1 - p.core).wait_recv()
        for step in range(p.chips):
            self.own(step).wait_send()
        for step in range(1, p.chips):
            self.relay(step, p.core).wait_send()


def spread_sems(parts, chips):
    return [pltpu.SemaphoreType.DMA((parts, chips)) for _ in range(4)]


def group_kernel(ctx_count, fsdp_count, src, out, *sems):
    place = Place(ctx_count, fsdp_count)
    greet(place.group_targets())
    spread = Spread(place, src, out, 0, sems[:4], 0)
    spread.start()
    local = pltpu.make_async_copy(src, out.at[place.me], sems[4])
    local.start()
    spread.forward()
    spread.end()
    local.wait()


def group_gather(values, ctx_count, fsdp_count, identity):
    rows, columns = values.shape
    gathered = pl.pallas_call(
        functools.partial(group_kernel, ctx_count, fsdp_count),
        out_shape=jax.ShapeDtypeStruct((fsdp_count, rows, columns), values.dtype),
        in_specs=[pl.BlockSpec(memory_space=pl.ANY)],
        out_specs=pl.BlockSpec(memory_space=pl.ANY),
        scratch_shapes=spread_sems(1, fsdp_count // 2) + [pltpu.SemaphoreType.DMA],
        compiler_params=pltpu.CompilerParams(
            collective_id=identity, has_side_effects=True, vmem_limit_bytes=VMEM_BYTES
        ),
    )(values)
    return gathered.reshape(fsdp_count * rows, columns)


def ctx_kernel(ctx_count, fsdp_count, src, out, send_sem, recv_sem, local_sem):
    place = Place(ctx_count, fsdp_count)
    greet(place.ctx_targets())

    def copy(step, slot):
        return remote(
            src,
            out.at[slot],
            send_sem.at[step],
            recv_sem.at[step],
            (place.ctx_ahead(step), place.me),
        )

    for step in range(1, ctx_count):
        copy(step, place.z).start()
    local = pltpu.make_async_copy(src, out.at[place.z], local_sem)
    local.start()
    for step in range(1, ctx_count):
        copy(step, place.ctx_behind(step)).wait_recv()
    for step in range(1, ctx_count):
        copy(step, place.z).wait_send()
    local.wait()


def ctx_gather(values, ctx_count, fsdp_count, identity):
    rows, columns = values.shape
    gathered = pl.pallas_call(
        functools.partial(ctx_kernel, ctx_count, fsdp_count),
        out_shape=jax.ShapeDtypeStruct((ctx_count, rows, columns), values.dtype),
        in_specs=[pl.BlockSpec(memory_space=pl.ANY)],
        out_specs=pl.BlockSpec(memory_space=pl.ANY),
        scratch_shapes=[
            pltpu.SemaphoreType.DMA((ctx_count,)),
            pltpu.SemaphoreType.DMA((ctx_count,)),
            pltpu.SemaphoreType.DMA,
        ],
        compiler_params=pltpu.CompilerParams(
            collective_id=identity, has_side_effects=True, vmem_limit_bytes=VMEM_BYTES
        ),
    )(values)
    return gathered.reshape(ctx_count * rows, columns)


def scatter_sum(place, partial, pair, stage, inbox, sems):
    pair_send, pair_recv, send, recv = sems
    chips = place.chips

    def swap(step):
        return remote(
            partial.at[place.ahead(step) + 1 - place.core],
            pair.at[step],
            pair_send.at[step],
            pair_recv.at[step],
            (place.z, place.sibling),
        )

    def give(step):
        return remote(
            stage.at[step],
            inbox.at[step],
            send.at[step],
            recv.at[step],
            (place.z, place.ahead(step) + place.core),
        )

    order = list(range(1, chips)) + [0]
    for step in order:
        swap(step).start()
    for step in order:
        swap(step).wait_recv()
        if step > 0:
            both = partial[place.ahead(step) + place.core].astype(jnp.float32) + pair[step].astype(
                jnp.float32
            )
            stage[step] = both.astype(jnp.bfloat16)
            give(step).start()
    result = partial[place.me].astype(jnp.float32) + pair[0].astype(jnp.float32)
    for step in range(1, chips):
        give(step).wait_recv()
        result = result + inbox[step].astype(jnp.float32)
    for step in order:
        swap(step).wait_send()
        if step > 0:
            give(step).wait_send()
    return result


def scatter_scratch(chips, rows, columns):
    return [pltpu.VMEM((chips, rows, columns), jnp.bfloat16) for _ in range(3)] + [
        pltpu.SemaphoreType.DMA((chips,)) for _ in range(4)
    ]


def renoise_kernel(
    ctx_count, fsdp_count, partial, mixed, noise, sig, generated, noisy, out, *scratch
):
    place = Place(ctx_count, fsdp_count)
    greet(place.group_targets())
    gen_sum = scatter_sum(place, partial, *scratch[:3], scratch[3:7])
    value = (mixed[...].astype(jnp.float32) + gen_sum).astype(jnp.bfloat16)
    generated[...] = value
    level = sig[:, :1]
    noisy[...] = (
        (1.0 - level) * value.astype(jnp.float32) + level * noise[...].astype(jnp.float32)
    ).astype(jnp.bfloat16)
    spread = Spread(place, noisy, out, 0, scratch[7:11], 0)
    spread.start()
    local = pltpu.make_async_copy(noisy, out.at[place.me], scratch[11])
    local.start()
    spread.forward()
    spread.end()
    local.wait()


def cotangent_kernel(
    ctx_count, fsdp_count, partial, generated, noisy, out, cotangent, *scratch
):
    place = Place(ctx_count, fsdp_count)
    greet(place.group_targets() + place.ctx_targets())
    teacher_sum = scatter_sum(place, partial, *scratch[:3], scratch[3:7])
    real = noisy[...].astype(jnp.float32) + teacher_sum
    cotangent[...] = (generated[...].astype(jnp.float32) - real).astype(jnp.bfloat16)
    ctx_send, ctx_recv, local_sem = scratch[11:14]

    def along(step, source):
        return remote(
            cotangent,
            out.at[source * fsdp_count + place.me],
            ctx_send.at[step],
            ctx_recv.at[step],
            (place.ctx_ahead(step), place.me),
        )

    for step in range(1, ctx_count):
        along(step, place.z).start()
    spreads = [Spread(place, cotangent, out, place.z * fsdp_count, scratch[7:11], 0)]
    spreads[0].start()
    local = pltpu.make_async_copy(cotangent, out.at[place.z * fsdp_count + place.me], local_sem)
    local.start()
    for step in range(1, ctx_count):
        source = place.ctx_behind(step)
        along(step, source).wait_recv()
        row = source * fsdp_count
        spreads.append(
            Spread(place, out.at[row + place.me], out, row, scratch[7:11], step)
        )
        spreads[-1].start()
        spreads[-2].forward()
    spreads[-1].forward()
    for spread in spreads:
        spread.end()
    for step in range(1, ctx_count):
        along(step, place.z).wait_send()
    local.wait()


def renoise(partial, mixed, noise, sig, ctx_count, fsdp_count, identity):
    rows, columns = mixed.shape
    chips = fsdp_count // 2
    vmem = pl.BlockSpec(memory_space=pltpu.VMEM)
    block = jax.ShapeDtypeStruct((rows, columns), jnp.bfloat16)
    generated, noisy, gathered = pl.pallas_call(
        functools.partial(renoise_kernel, ctx_count, fsdp_count),
        out_shape=(
            block,
            block,
            jax.ShapeDtypeStruct((fsdp_count, rows, columns), jnp.bfloat16),
        ),
        in_specs=[vmem] * 4,
        out_specs=(vmem, vmem, pl.BlockSpec(memory_space=pl.ANY)),
        scratch_shapes=scatter_scratch(chips, rows, columns)
        + spread_sems(1, chips)
        + [pltpu.SemaphoreType.DMA],
        compiler_params=pltpu.CompilerParams(
            collective_id=identity, has_side_effects=True, vmem_limit_bytes=VMEM_BYTES
        ),
    )(
        partial.reshape(fsdp_count, rows, columns),
        mixed,
        noise,
        jnp.broadcast_to(sig, (rows, 128)),
    )
    return generated, noisy, gathered.reshape(fsdp_count * rows, columns)


def all_cotangents(partial, generated, noisy, ctx_count, fsdp_count, identity):
    rows, columns = noisy.shape
    chips = fsdp_count // 2
    vmem = pl.BlockSpec(memory_space=pltpu.VMEM)
    devices = ctx_count * fsdp_count
    gathered = pl.pallas_call(
        functools.partial(cotangent_kernel, ctx_count, fsdp_count),
        out_shape=jax.ShapeDtypeStruct((devices, rows, columns), jnp.bfloat16),
        in_specs=[vmem] * 3,
        out_specs=pl.BlockSpec(memory_space=pl.ANY),
        scratch_shapes=[pltpu.VMEM((rows, columns), jnp.bfloat16)]
        + scatter_scratch(chips, rows, columns)
        + spread_sems(ctx_count, chips)
        + [
            pltpu.SemaphoreType.DMA((ctx_count,)),
            pltpu.SemaphoreType.DMA((ctx_count,)),
            pltpu.SemaphoreType.DMA,
        ],
        compiler_params=pltpu.CompilerParams(
            collective_id=identity, has_side_effects=True, vmem_limit_bytes=VMEM_BYTES
        ),
    )(partial.reshape(fsdp_count, rows, columns), generated, noisy)
    return gathered.reshape(devices * rows, columns)


def per_device(
    clean,
    noise,
    noise_two,
    steps_gen,
    steps_teacher,
    cache_key,
    cache_value,
    cache_block,
    span_block,
    gen_query,
    gen_key,
    gen_value,
    gen_out,
    teacher_query,
    teacher_key,
    teacher_value,
    teacher_out,
):
    ctx_count = lax.axis_size("ctx")
    fsdp_count = lax.axis_size("fsdp")
    tok_dev = clean.shape[0]
    block_rows = tok_dev * fsdp_count
    total = block_rows * ctx_count
    offset = (lax.axis_index("ctx") * fsdp_count + lax.axis_index("fsdp")) * tok_dev
    width = gen_query.shape[1]
    heads = width // HEAD
    sig_gen = sigmas(steps_gen, offset, tok_dev, total)
    mixed = (
        (1.0 - sig_gen) * clean.astype(jnp.float32) + sig_gen * noise.astype(jnp.float32)
    ).astype(jnp.bfloat16)
    slots = cache_block.shape[0]
    visible = (cache_block < span_block[0]).astype(jnp.bfloat16)
    flag_rows = -(-slots // (16 * width)) * 16
    flags = jnp.pad(visible, (0, flag_rows * width - slots)).reshape(flag_rows, width)
    cache = lax.all_gather(
        jnp.concatenate([cache_key, cache_value, flags], axis=0), "ctx", axis=0, tiled=False
    )
    gen_stack = jnp.concatenate([gen_query, gen_key, gen_value], axis=1)
    projected = jnp.dot(
        normed(group_gather(mixed, ctx_count, fsdp_count, 0)),
        gen_stack,
        preferred_element_type=jnp.float32,
    ).astype(jnp.bfloat16)
    query_heads = projected[:, :width].reshape(block_rows, heads, HEAD)
    span = ctx_gather(projected[:, width:], ctx_count, fsdp_count, 1)
    slots_all = slots * ctx_count
    cached_keys = cache[:, :slots].reshape(slots_all, heads, HEAD)
    cached_values = cache[:, slots : 2 * slots].reshape(slots_all, heads, HEAD)
    allowed = cache[:, 2 * slots :].reshape(ctx_count, -1)[:, :slots].reshape(-1) > 0
    attn = attend(
        query_heads,
        (
            (cached_keys, cached_values, allowed),
            (
                span[:, :width].reshape(total, heads, HEAD),
                span[:, width:].reshape(total, heads, HEAD),
                None,
            ),
        ),
    )
    attn_all = lax.all_gather(attn, "ctx", axis=0, tiled=True)
    sig_teacher = sigmas(steps_teacher, offset, tok_dev, total)
    generated, noisy, noisy_group = renoise(
        jnp.dot(attn, gen_out, preferred_element_type=jnp.float32).astype(jnp.bfloat16),
        mixed,
        noise_two,
        sig_teacher,
        ctx_count,
        fsdp_count,
        2,
    )
    teacher_stack = jnp.concatenate([teacher_query, teacher_key, teacher_value], axis=1)
    teacher_proj = jnp.dot(
        normed(noisy_group),
        teacher_stack,
        preferred_element_type=jnp.float32,
    ).astype(jnp.bfloat16)
    teacher_heads = teacher_proj[:, :width].reshape(block_rows, heads, HEAD)
    t_span = ctx_gather(teacher_proj[:, width:], ctx_count, fsdp_count, 3)
    teacher_attn = attend(
        teacher_heads,
        (
            (
                t_span[:, :width].reshape(total, heads, HEAD),
                t_span[:, width:].reshape(total, heads, HEAD),
                None,
            ),
        ),
    )
    cotangents = all_cotangents(
        jnp.dot(teacher_attn, teacher_out, preferred_element_type=jnp.float32).astype(jnp.bfloat16),
        generated,
        noisy,
        ctx_count,
        fsdp_count,
        4,
    )
    grad_out = lax.dot_general(
        attn_all,
        cotangents,
        (((0,), (0,)), ((), ())),
        preferred_element_type=jnp.float32,
    ).astype(jnp.bfloat16)
    return (generated, grad_out)


def solution(mesh):
    in_specs = (
        P(("ctx", "fsdp"), None),
        P(("ctx", "fsdp"), None),
        P(("ctx", "fsdp"), None),
        P(),
        P(),
        P("ctx", "fsdp"),
        P("ctx", "fsdp"),
        P("ctx"),
        P(),
        P(None, "fsdp"),
        P(None, "fsdp"),
        P(None, "fsdp"),
        P("fsdp", None),
        P(None, "fsdp"),
        P(None, "fsdp"),
        P(None, "fsdp"),
        P("fsdp", None),
    )
    out_specs = (P(("ctx", "fsdp"), None), P("fsdp", None))
    return jax.shard_map(
        per_device, mesh=mesh, in_specs=in_specs, out_specs=out_specs, check_vma=False
    )
```

```python
import functools

import jax
import jax.numpy as jnp
from jax import lax
from jax.experimental import pallas as pl
from jax.experimental.pallas import tpu as pltpu
from jax.sharding import PartitionSpec as P

HEAD = 128
FRAMES = 3
STEPS = 1000


SHIFT = 5.0
EPS = 1e-06


def sigmas(steps, offset, count, total):
    level = 1.0 - steps.astype(jnp.float32) / STEPS
    sig = SHIFT * level / (1.0 + (SHIFT - 1.0) * level)
    positions = offset + jnp.arange(count, dtype=jnp.int32)
    frame = positions * FRAMES // total
    match = (frame[:, None] == jnp.arange(FRAMES, dtype=jnp.int32)[None, :]).astype(jnp.float32)
    return jnp.sum(match * sig[None, :], axis=1)[:, None]


def normed(values):
    wide = values.astype(jnp.float32)
    return (wide * lax.rsqrt(jnp.mean(wide * wide, axis=1, keepdims=True) + EPS)).astype(
        jnp.bfloat16
    )


def attend(query_heads, parts):
    head_size = query_heads.shape[2]
    scale = 1.0 / head_size**0.5
    all_scores = []
    for keys, _, allowed in parts:
        scores = (
            jnp.einsum("rhd,phd->hrp", query_heads, keys, preferred_element_type=jnp.float32)
            * scale
        )
        if allowed is not None:
            scores = jnp.where(allowed[None, None, :], scores, -1e30)
        all_scores.append(scores)
    top = all_scores[0].max(axis=2)
    for scores in all_scores[1:]:
        top = jnp.maximum(top, scores.max(axis=2))
    total = 0.0
    accum = 0.0
    for scores, (_, values, allowed) in zip(all_scores, parts):
        weights = jnp.exp(scores - top[:, :, None])
        if allowed is not None:
            weights = jnp.where(allowed[None, None, :], weights, 0.0)
        total = total + weights.sum(axis=2)
        accum = accum + jnp.einsum(
            "hrp,phd->hrd",
            weights.astype(jnp.bfloat16),
            values,
            preferred_element_type=jnp.float32,
        )
    heads, rows, _ = accum.shape
    result = accum / total[:, :, None]
    return jnp.transpose(result, (1, 0, 2)).reshape(rows, heads * head_size).astype(jnp.bfloat16)


MESH = pl.DeviceIdType.MESH
VMEM_BYTES = 40 * 1024 * 1024


class Place:
    def __init__(self, ctx_count, fsdp_count):
        self.ctx_count = ctx_count
        self.count = fsdp_count
        self.chips = fsdp_count // 2
        self.z = lax.axis_index("ctx")
        self.me = lax.axis_index("fsdp")
        self.chip = lax.div(self.me, 2)
        self.core = lax.rem(self.me, 2)
        self.sibling = self.chip * 2 + 1 - self.core

    def across(self, step):
        x, y = lax.rem(self.chip, 2), lax.div(self.chip, 2)
        x = 1 - x if step in (1, 3) else x
        y = 1 - y if step in (2, 3) else y
        return (y * 2 + x) * 2

    def ahead(self, step):
        if self.chips == 4:
            return self.across(step)
        return lax.rem(self.chip + step, self.chips) * 2

    def behind(self, step):
        if self.chips == 4:
            return self.across(step)
        return lax.rem(self.chip + self.chips - step, self.chips) * 2

    def group_targets(self):
        same_core = [(self.z, self.ahead(j) + self.core) for j in range(1, self.chips)]
        return same_core + [(self.z, self.sibling)]

    def ctx_ahead(self, step):
        return lax.rem(self.z + step, self.ctx_count)

    def ctx_behind(self, step):
        return lax.rem(self.z + self.ctx_count - step, self.ctx_count)

    def ctx_targets(self):
        return [(self.ctx_ahead(i), self.me) for i in range(1, self.ctx_count)]


def greet(targets):
    barrier = pltpu.get_barrier_semaphore()
    for target in targets:
        pl.semaphore_signal(barrier, inc=1, device_id=target, device_id_type=MESH)
    pl.semaphore_wait(barrier, len(targets))


def remote(src, dst, send_sem, recv_sem, target):
    return pltpu.make_async_remote_copy(
        src_ref=src,
        dst_ref=dst,
        send_sem=send_sem,
        recv_sem=recv_sem,
        device_id=target,
        device_id_type=MESH,
    )


class Spread:
    def __init__(self, place, src, out, row, sems, index):
        self.place, self.src, self.out, self.row = place, src, out, row
        self.send, self.recv, self.relay_send, self.relay_recv = (s.at[index] for s in sems)
        self.half = out.shape[1] // 2
        self.square = place.chips == 4 and self.half % 16 == 0
        self.direct = range(1, 3) if self.square else range(1, place.chips)

    def own(self, step):
        p = self.place
        target = (p.z, p.sibling if step == 0 else p.ahead(step) + p.core)
        return remote(
            self.src, self.out.at[self.row + p.me], self.send.at[step], self.recv.at[step], target
        )

    def arrival(self, step):
        p = self.place
        source = p.sibling if step == 0 else p.behind(step) + p.core
        return remote(
            self.src,
            self.out.at[self.row + source],
            self.send.at[step],
            self.recv.at[step],
            (p.z, p.sibling),
        )

    def relay(self, step, core):
        p = self.place
        block = self.out.at[self.row + p.behind(step) + core]
        return remote(
            block, block, self.relay_send.at[step], self.relay_recv.at[step], (p.z, p.sibling)
        )

    def start(self):
        for step in list(self.direct) + [0]:
            self.own(step).start()

    def hop(self, step, origin):
        p = self.place
        part = pl.ds((step - 1) * self.half, self.half)
        block = self.out.at[self.row + p.across(origin) + p.core, part]
        return remote(
            block,
            block,
            self.send.at[2 + step],
            self.recv.at[2 + step],
            (p.z, p.across(3 - step) + p.core),
        )

    def forward(self):
        for step in self.direct:
            self.arrival(step).wait_recv()
            if self.square:
                self.hop(step, step).start()
            self.relay(step, self.place.core).start()

    def corner(self):
        if self.square:
            self.hop(1, 3).wait_recv()
            self.hop(2, 3).wait_recv()
            self.relay(3, self.place.core).start()

    def end(self):
        p = self.place
        self.arrival(0).wait_recv()
        for step in range(1, p.chips):
            self.relay(step, 1 - p.core).wait_recv()
        for step in [0] + list(self.direct):
            self.own(step).wait_send()
            if self.square and step > 0:
                self.hop(step, step).wait_send()
        for step in range(1, p.chips):
            self.relay(step, p.core).wait_send()


def spread_sems(parts, chips):
    return [pltpu.SemaphoreType.DMA((parts, chips + 1)) for _ in range(4)]


def group_kernel(ctx_count, fsdp_count, src, out, *sems):
    place = Place(ctx_count, fsdp_count)
    greet(place.group_targets())
    spread = Spread(place, src, out, 0, sems[:4], 0)
    spread.start()
    local = pltpu.make_async_copy(src, out.at[place.me], sems[4])
    local.start()
    spread.forward()
    spread.corner()
    spread.end()
    local.wait()


def group_gather(values, ctx_count, fsdp_count, identity):
    rows, columns = values.shape
    gathered = pl.pallas_call(
        functools.partial(group_kernel, ctx_count, fsdp_count),
        out_shape=jax.ShapeDtypeStruct((fsdp_count, rows, columns), values.dtype),
        in_specs=[pl.BlockSpec(memory_space=pl.ANY)],
        out_specs=pl.BlockSpec(memory_space=pl.ANY),
        scratch_shapes=spread_sems(1, fsdp_count // 2) + [pltpu.SemaphoreType.DMA],
        compiler_params=pltpu.CompilerParams(
            collective_id=identity, has_side_effects=True, vmem_limit_bytes=VMEM_BYTES
        ),
    )(values)
    return gathered.reshape(fsdp_count * rows, columns)


def ctx_kernel(
    ctx_count, fsdp_count, src, out, right_send, right_recv, left_send, left_recv, local_sem
):
    place = Place(ctx_count, fsdp_count)
    z, last = place.z, ctx_count - 1
    greet(place.ctx_targets())
    half = src.shape[0] // 2
    local = pltpu.make_async_copy(src, out.at[z], local_sem)
    local.start()

    def right(hops, part, slot):
        rows = pl.ds(part * half, half)
        block = src.at[rows] if hops == 0 else out.at[slot, rows]
        return remote(
            block,
            out.at[slot, rows],
            right_send.at[hops, part],
            right_recv.at[hops, part],
            (place.ctx_ahead(1), place.me),
        )

    def left(hops, part, slot):
        rows = pl.ds(part * half, half)
        block = src.at[rows] if hops == 0 else out.at[slot, rows]
        return remote(
            block,
            out.at[slot, rows],
            left_send.at[hops, part],
            left_recv.at[hops, part],
            (place.ctx_behind(1), place.me),
        )

    for hops in range(ctx_count):
        for part in range(2):
            if hops > 0:

                @pl.when(z >= hops)
                def _():
                    right(hops - 1, part, z - hops).wait_recv()

                @pl.when(z + hops <= last)
                def _():
                    left(hops - 1, part, z + hops).wait_recv()

            if hops < last:

                @pl.when(jnp.logical_and(z >= hops, z < last))
                def _():
                    right(hops, part, z - hops).start()

                @pl.when(jnp.logical_and(z + hops <= last, z > 0))
                def _():
                    left(hops, part, z + hops).start()

    for hops in range(last):
        for part in range(2):

            @pl.when(jnp.logical_and(z >= hops, z < last))
            def _():
                right(hops, part, z - hops).wait_send()

            @pl.when(jnp.logical_and(z + hops <= last, z > 0))
            def _():
                left(hops, part, z + hops).wait_send()

    local.wait()


def ctx_gather(values, ctx_count, fsdp_count, identity):
    rows, columns = values.shape
    gathered = pl.pallas_call(
        functools.partial(ctx_kernel, ctx_count, fsdp_count),
        out_shape=jax.ShapeDtypeStruct((ctx_count, rows, columns), values.dtype),
        in_specs=[pl.BlockSpec(memory_space=pl.ANY)],
        out_specs=pl.BlockSpec(memory_space=pl.ANY),
        scratch_shapes=[
            pltpu.SemaphoreType.DMA((ctx_count, 2)),
            pltpu.SemaphoreType.DMA((ctx_count, 2)),
            pltpu.SemaphoreType.DMA((ctx_count, 2)),
            pltpu.SemaphoreType.DMA((ctx_count, 2)),
            pltpu.SemaphoreType.DMA,
        ],
        compiler_params=pltpu.CompilerParams(
            collective_id=identity, has_side_effects=True, vmem_limit_bytes=VMEM_BYTES
        ),
    )(values)
    return gathered.reshape(ctx_count * rows, columns)


def scatter_sum(place, partial, pair, stage, inbox, sems):
    pair_send, pair_recv, send, recv = sems
    chips = place.chips

    def swap(step):
        return remote(
            partial.at[place.ahead(step) + 1 - place.core],
            pair.at[step],
            pair_send.at[step],
            pair_recv.at[step],
            (place.z, place.sibling),
        )

    def give(step):
        return remote(
            stage.at[step],
            inbox.at[step],
            send.at[step],
            recv.at[step],
            (place.z, place.ahead(step) + place.core),
        )

    order = list(range(1, chips)) + [0]
    for step in order:
        swap(step).start()
    for step in order:
        swap(step).wait_recv()
        if step > 0:
            both = partial[place.ahead(step) + place.core].astype(jnp.float32) + pair[step].astype(
                jnp.float32
            )
            stage[step] = both.astype(jnp.bfloat16)
            give(step).start()
    result = partial[place.me].astype(jnp.float32) + pair[0].astype(jnp.float32)
    for step in range(1, chips):
        give(step).wait_recv()
        result = result + inbox[step].astype(jnp.float32)
    for step in order:
        swap(step).wait_send()
        if step > 0:
            give(step).wait_send()
    return result


def scatter_scratch(chips, rows, columns):
    return [pltpu.VMEM((chips, rows, columns), jnp.bfloat16) for _ in range(3)] + [
        pltpu.SemaphoreType.DMA((chips,)) for _ in range(4)
    ]


def renoise_kernel(
    ctx_count, fsdp_count, partial, mixed, noise, sig, generated, noisy, out, *scratch
):
    place = Place(ctx_count, fsdp_count)
    greet(place.group_targets())
    gen_sum = scatter_sum(place, partial, *scratch[:3], scratch[3:7])
    value = (mixed[...].astype(jnp.float32) + gen_sum).astype(jnp.bfloat16)
    generated[...] = value
    level = sig[:, :1]
    noisy[...] = (
        (1.0 - level) * value.astype(jnp.float32) + level * noise[...].astype(jnp.float32)
    ).astype(jnp.bfloat16)
    spread = Spread(place, noisy, out, 0, scratch[7:11], 0)
    spread.start()
    local = pltpu.make_async_copy(noisy, out.at[place.me], scratch[11])
    local.start()
    spread.forward()
    spread.corner()
    spread.end()
    local.wait()


def cotangent_kernel(
    ctx_count, fsdp_count, partial, generated, noisy, out, cotangent, *scratch
):
    place = Place(ctx_count, fsdp_count)
    greet(place.group_targets() + place.ctx_targets())
    teacher_sum = scatter_sum(place, partial, *scratch[:3], scratch[3:7])
    real = noisy[...].astype(jnp.float32) + teacher_sum
    cotangent[...] = (generated[...].astype(jnp.float32) - real).astype(jnp.bfloat16)
    ctx_send, ctx_recv, local_sem = scratch[11:14]

    def along(step, source):
        return remote(
            cotangent,
            out.at[source * fsdp_count + place.me],
            ctx_send.at[step],
            ctx_recv.at[step],
            (place.ctx_ahead(step), place.me),
        )

    for step in range(1, ctx_count):
        along(step, place.z).start()
    spreads = [Spread(place, cotangent, out, place.z * fsdp_count, scratch[7:11], 0)]
    spreads[0].start()
    local = pltpu.make_async_copy(cotangent, out.at[place.z * fsdp_count + place.me], local_sem)
    local.start()
    for step in range(1, ctx_count):
        source = place.ctx_behind(step)
        along(step, source).wait_recv()
        row = source * fsdp_count
        spreads.append(
            Spread(place, out.at[row + place.me], out, row, scratch[7:11], step)
        )
        spreads[-1].start()
        spreads[-2].forward()
        if step > 1:
            spreads[-3].corner()
    spreads[-1].forward()
    for spread in spreads[-2:]:
        spread.corner()
    for spread in spreads:
        spread.end()
    for step in range(1, ctx_count):
        along(step, place.z).wait_send()
    local.wait()


def renoise(partial, mixed, noise, sig, ctx_count, fsdp_count, identity):
    rows, columns = mixed.shape
    chips = fsdp_count // 2
    vmem = pl.BlockSpec(memory_space=pltpu.VMEM)
    block = jax.ShapeDtypeStruct((rows, columns), jnp.bfloat16)
    generated, noisy, gathered = pl.pallas_call(
        functools.partial(renoise_kernel, ctx_count, fsdp_count),
        out_shape=(
            block,
            block,
            jax.ShapeDtypeStruct((fsdp_count, rows, columns), jnp.bfloat16),
        ),
        in_specs=[vmem] * 4,
        out_specs=(vmem, vmem, pl.BlockSpec(memory_space=pl.ANY)),
        scratch_shapes=scatter_scratch(chips, rows, columns)
        + spread_sems(1, chips)
        + [pltpu.SemaphoreType.DMA],
        compiler_params=pltpu.CompilerParams(
            collective_id=identity, has_side_effects=True, vmem_limit_bytes=VMEM_BYTES
        ),
    )(
        partial.reshape(fsdp_count, rows, columns),
        mixed,
        noise,
        jnp.broadcast_to(sig, (rows, 128)),
    )
    return generated, noisy, gathered.reshape(fsdp_count * rows, columns)


def all_cotangents(partial, generated, noisy, ctx_count, fsdp_count, identity):
    rows, columns = noisy.shape
    chips = fsdp_count // 2
    vmem = pl.BlockSpec(memory_space=pltpu.VMEM)
    devices = ctx_count * fsdp_count
    gathered = pl.pallas_call(
        functools.partial(cotangent_kernel, ctx_count, fsdp_count),
        out_shape=jax.ShapeDtypeStruct((devices, rows, columns), jnp.bfloat16),
        in_specs=[vmem] * 3,
        out_specs=pl.BlockSpec(memory_space=pl.ANY),
        scratch_shapes=[pltpu.VMEM((rows, columns), jnp.bfloat16)]
        + scatter_scratch(chips, rows, columns)
        + spread_sems(ctx_count, chips)
        + [
            pltpu.SemaphoreType.DMA((ctx_count,)),
            pltpu.SemaphoreType.DMA((ctx_count,)),
            pltpu.SemaphoreType.DMA,
        ],
        compiler_params=pltpu.CompilerParams(
            collective_id=identity, has_side_effects=True, vmem_limit_bytes=VMEM_BYTES
        ),
    )(partial.reshape(fsdp_count, rows, columns), generated, noisy)
    return gathered.reshape(devices * rows, columns)


def per_device(
    clean,
    noise,
    noise_two,
    steps_gen,
    steps_teacher,
    cache_key,
    cache_value,
    cache_block,
    span_block,
    gen_query,
    gen_key,
    gen_value,
    gen_out,
    teacher_query,
    teacher_key,
    teacher_value,
    teacher_out,
):
    ctx_count = lax.axis_size("ctx")
    fsdp_count = lax.axis_size("fsdp")
    tok_dev = clean.shape[0]
    block_rows = tok_dev * fsdp_count
    total = block_rows * ctx_count
    offset = (lax.axis_index("ctx") * fsdp_count + lax.axis_index("fsdp")) * tok_dev
    width = gen_query.shape[1]
    heads = width // HEAD
    sig_gen = sigmas(steps_gen, offset, tok_dev, total)
    mixed = (
        (1.0 - sig_gen) * clean.astype(jnp.float32) + sig_gen * noise.astype(jnp.float32)
    ).astype(jnp.bfloat16)
    slots = cache_block.shape[0]
    visible = (cache_block < span_block[0]).astype(jnp.bfloat16)
    flag_rows = -(-slots // (16 * width)) * 16
    flags = jnp.pad(visible, (0, flag_rows * width - slots)).reshape(flag_rows, width)
    cache = lax.all_gather(
        jnp.concatenate([cache_key, cache_value, flags], axis=0), "ctx", axis=0, tiled=False
    )
    gen_stack = jnp.concatenate([gen_query, gen_key, gen_value], axis=1)
    projected = jnp.dot(
        normed(group_gather(mixed, ctx_count, fsdp_count, 0)),
        gen_stack,
        preferred_element_type=jnp.float32,
    ).astype(jnp.bfloat16)
    query_heads = projected[:, :width].reshape(block_rows, heads, HEAD)
    span = ctx_gather(projected[:, width:], ctx_count, fsdp_count, 1)
    slots_all = slots * ctx_count
    cached_keys = cache[:, :slots].reshape(slots_all, heads, HEAD)
    cached_values = cache[:, slots : 2 * slots].reshape(slots_all, heads, HEAD)
    allowed = cache[:, 2 * slots :].reshape(ctx_count, -1)[:, :slots].reshape(-1) > 0
    attn = attend(
        query_heads,
        (
            (cached_keys, cached_values, allowed),
            (
                span[:, :width].reshape(total, heads, HEAD),
                span[:, width:].reshape(total, heads, HEAD),
                None,
            ),
        ),
    )
    attn_all = lax.all_gather(attn, "ctx", axis=0, tiled=True)
    sig_teacher = sigmas(steps_teacher, offset, tok_dev, total)
    generated, noisy, noisy_group = renoise(
        jnp.dot(attn, gen_out, preferred_element_type=jnp.float32).astype(jnp.bfloat16),
        mixed,
        noise_two,
        sig_teacher,
        ctx_count,
        fsdp_count,
        2,
    )
    teacher_stack = jnp.concatenate([teacher_query, teacher_key, teacher_value], axis=1)
    teacher_proj = jnp.dot(
        normed(noisy_group),
        teacher_stack,
        preferred_element_type=jnp.float32,
    ).astype(jnp.bfloat16)
    teacher_heads = teacher_proj[:, :width].reshape(block_rows, heads, HEAD)
    t_span = ctx_gather(teacher_proj[:, width:], ctx_count, fsdp_count, 3)
    teacher_attn = attend(
        teacher_heads,
        (
            (
                t_span[:, :width].reshape(total, heads, HEAD),
                t_span[:, width:].reshape(total, heads, HEAD),
                None,
            ),
        ),
    )
    cotangents = all_cotangents(
        jnp.dot(teacher_attn, teacher_out, preferred_element_type=jnp.float32).astype(jnp.bfloat16),
        generated,
        noisy,
        ctx_count,
        fsdp_count,
        4,
    )
    grad_out = lax.dot_general(
        attn_all,
        cotangents,
        (((0,), (0,)), ((), ())),
        preferred_element_type=jnp.float32,
    ).astype(jnp.bfloat16)
    return (generated, grad_out)


def solution(mesh):
    in_specs = (
        P(("ctx", "fsdp"), None),
        P(("ctx", "fsdp"), None),
        P(("ctx", "fsdp"), None),
        P(),
        P(),
        P("ctx", "fsdp"),
        P("ctx", "fsdp"),
        P("ctx"),
        P(),
        P(None, "fsdp"),
        P(None, "fsdp"),
        P(None, "fsdp"),
        P("fsdp", None),
        P(None, "fsdp"),
        P(None, "fsdp"),
        P(None, "fsdp"),
        P("fsdp", None),
    )
    out_specs = (P(("ctx", "fsdp"), None), P("fsdp", None))
    return jax.shard_map(
        per_device, mesh=mesh, in_specs=in_specs, out_specs=out_specs, check_vma=False
    )
```

```python
import functools

import jax
import jax.numpy as jnp
from jax import lax
from jax.experimental import pallas as pl
from jax.experimental.pallas import tpu as pltpu
from jax.sharding import PartitionSpec as P

HEAD = 128
FRAMES = 3
STEPS = 1000


SHIFT = 5.0
EPS = 1e-06


def sigmas(steps, offset, count, total):
    level = 1.0 - steps.astype(jnp.float32) / STEPS
    sig = SHIFT * level / (1.0 + (SHIFT - 1.0) * level)
    positions = offset + jnp.arange(count, dtype=jnp.int32)
    frame = positions * FRAMES // total
    match = (frame[:, None] == jnp.arange(FRAMES, dtype=jnp.int32)[None, :]).astype(jnp.float32)
    return jnp.sum(match * sig[None, :], axis=1)[:, None]


def normed(values):
    wide = values.astype(jnp.float32)
    return (wide * lax.rsqrt(jnp.mean(wide * wide, axis=1, keepdims=True) + EPS)).astype(
        jnp.bfloat16
    )


def attend(query_heads, parts):
    head_size = query_heads.shape[2]
    scale = 1.0 / head_size**0.5
    all_scores = []
    for keys, _, allowed in parts:
        scores = (
            jnp.einsum("rhd,phd->hrp", query_heads, keys, preferred_element_type=jnp.float32)
            * scale
        )
        if allowed is not None:
            scores = jnp.where(allowed[None, None, :], scores, -1e30)
        all_scores.append(scores)
    top = all_scores[0].max(axis=2)
    for scores in all_scores[1:]:
        top = jnp.maximum(top, scores.max(axis=2))
    total = 0.0
    accum = 0.0
    for scores, (_, values, allowed) in zip(all_scores, parts):
        weights = jnp.exp(scores - top[:, :, None])
        if allowed is not None:
            weights = jnp.where(allowed[None, None, :], weights, 0.0)
        total = total + weights.sum(axis=2)
        accum = accum + jnp.einsum(
            "hrp,phd->hrd",
            weights.astype(jnp.bfloat16),
            values,
            preferred_element_type=jnp.float32,
        )
    heads, rows, _ = accum.shape
    result = accum / total[:, :, None]
    return jnp.transpose(result, (1, 0, 2)).reshape(rows, heads * head_size).astype(jnp.bfloat16)


MESH = pl.DeviceIdType.MESH
VMEM_BYTES = 40 * 1024 * 1024


class Place:
    def __init__(self, ctx_count, fsdp_count):
        self.ctx_count = ctx_count
        self.count = fsdp_count
        self.chips = fsdp_count // 2
        self.z = lax.axis_index("ctx")
        self.me = lax.axis_index("fsdp")
        self.chip = lax.div(self.me, 2)
        self.core = lax.rem(self.me, 2)
        self.sibling = self.chip * 2 + 1 - self.core

    def across(self, step):
        x, y = lax.rem(self.chip, 2), lax.div(self.chip, 2)
        x = 1 - x if step in (1, 3) else x
        y = 1 - y if step in (2, 3) else y
        return (y * 2 + x) * 2

    def ahead(self, step):
        if self.chips == 4:
            return self.across(step)
        return lax.rem(self.chip + step, self.chips) * 2

    def behind(self, step):
        if self.chips == 4:
            return self.across(step)
        return lax.rem(self.chip + self.chips - step, self.chips) * 2

    def group_targets(self):
        same_core = [(self.z, self.ahead(j) + self.core) for j in range(1, self.chips)]
        return same_core + [(self.z, self.sibling)]

    def ctx_ahead(self, step):
        return lax.rem(self.z + step, self.ctx_count)

    def ctx_behind(self, step):
        return lax.rem(self.z + self.ctx_count - step, self.ctx_count)

    def ctx_targets(self):
        return [(self.ctx_ahead(i), self.me) for i in range(1, self.ctx_count)]


def greet(targets):
    barrier = pltpu.get_barrier_semaphore()
    for target in targets:
        pl.semaphore_signal(barrier, inc=1, device_id=target, device_id_type=MESH)
    pl.semaphore_wait(barrier, len(targets))


def remote(src, dst, send_sem, recv_sem, target):
    return pltpu.make_async_remote_copy(
        src_ref=src,
        dst_ref=dst,
        send_sem=send_sem,
        recv_sem=recv_sem,
        device_id=target,
        device_id_type=MESH,
    )


class Spread:
    def __init__(self, place, src, out, row, sems, index):
        self.place, self.src, self.out, self.row = place, src, out, row
        self.send, self.recv, self.relay_send, self.relay_recv = (s.at[index] for s in sems)
        self.half = out.shape[1] // 2
        self.square = place.chips == 4 and self.half % 16 == 0
        self.direct = range(1, 3) if self.square else range(1, place.chips)

    def own(self, step):
        p = self.place
        target = (p.z, p.sibling if step == 0 else p.ahead(step) + p.core)
        return remote(
            self.src, self.out.at[self.row + p.me], self.send.at[step], self.recv.at[step], target
        )

    def arrival(self, step):
        p = self.place
        source = p.sibling if step == 0 else p.behind(step) + p.core
        return remote(
            self.src,
            self.out.at[self.row + source],
            self.send.at[step],
            self.recv.at[step],
            (p.z, p.sibling),
        )

    def relay(self, step, core):
        p = self.place
        block = self.out.at[self.row + p.behind(step) + core]
        return remote(
            block, block, self.relay_send.at[step], self.relay_recv.at[step], (p.z, p.sibling)
        )

    def start(self):
        for step in list(self.direct) + [0]:
            self.own(step).start()

    def hop(self, step, origin):
        p = self.place
        part = pl.ds((step - 1) * self.half, self.half)
        block = self.out.at[self.row + p.across(origin) + p.core, part]
        return remote(
            block,
            block,
            self.send.at[2 + step],
            self.recv.at[2 + step],
            (p.z, p.across(3 - step) + p.core),
        )

    def forward(self):
        for step in self.direct:
            self.arrival(step).wait_recv()
            if self.square:
                self.hop(step, step).start()
            self.relay(step, self.place.core).start()

    def corner(self):
        if self.square:
            self.hop(1, 3).wait_recv()
            self.hop(2, 3).wait_recv()
            self.relay(3, self.place.core).start()

    def end(self):
        p = self.place
        self.arrival(0).wait_recv()
        for step in range(1, p.chips):
            self.relay(step, 1 - p.core).wait_recv()
        for step in [0] + list(self.direct):
            self.own(step).wait_send()
            if self.square and step > 0:
                self.hop(step, step).wait_send()
        for step in range(1, p.chips):
            self.relay(step, p.core).wait_send()


def spread_sems(parts, chips):
    return [pltpu.SemaphoreType.DMA((parts, chips + 1)) for _ in range(4)]


def group_kernel(ctx_count, fsdp_count, src, out, *sems):
    place = Place(ctx_count, fsdp_count)
    greet(place.group_targets())
    spread = Spread(place, src, out, 0, sems[:4], 0)
    spread.start()
    local = pltpu.make_async_copy(src, out.at[place.me], sems[4])
    local.start()
    spread.forward()
    spread.corner()
    spread.end()
    local.wait()


def group_gather(values, ctx_count, fsdp_count, identity):
    rows, columns = values.shape
    gathered = pl.pallas_call(
        functools.partial(group_kernel, ctx_count, fsdp_count),
        out_shape=jax.ShapeDtypeStruct((fsdp_count, rows, columns), values.dtype),
        in_specs=[pl.BlockSpec(memory_space=pl.ANY)],
        out_specs=pl.BlockSpec(memory_space=pl.ANY),
        scratch_shapes=spread_sems(1, fsdp_count // 2) + [pltpu.SemaphoreType.DMA],
        compiler_params=pltpu.CompilerParams(
            collective_id=identity, has_side_effects=True, vmem_limit_bytes=VMEM_BYTES
        ),
    )(values)
    return gathered.reshape(fsdp_count * rows, columns)


def ctx_kernel(
    ctx_count, fsdp_count, src, wide, weight, out, query, right_send, right_recv, left_send, left_recv, local_sem
):
    place = Place(ctx_count, fsdp_count)
    z, last = place.z, ctx_count - 1
    greet(place.ctx_targets())
    half = src.shape[0] // 2
    local = pltpu.make_async_copy(src, out.at[z], local_sem)
    local.start()

    def right(hops, part, slot):
        rows = pl.ds(part * half, half)
        block = src.at[rows] if hops == 0 else out.at[slot, rows]
        return remote(
            block,
            out.at[slot, rows],
            right_send.at[hops, part],
            right_recv.at[hops, part],
            (place.ctx_ahead(1), place.me),
        )

    def left(hops, part, slot):
        rows = pl.ds(part * half, half)
        block = src.at[rows] if hops == 0 else out.at[slot, rows]
        return remote(
            block,
            out.at[slot, rows],
            left_send.at[hops, part],
            left_recv.at[hops, part],
            (place.ctx_behind(1), place.me),
        )

    for hops in range(ctx_count):
        for part in range(2):
            if hops > 0:

                @pl.when(z >= hops)
                def _():
                    right(hops - 1, part, z - hops).wait_recv()

                @pl.when(z + hops <= last)
                def _():
                    left(hops - 1, part, z + hops).wait_recv()

            if hops < last:

                @pl.when(jnp.logical_and(z >= hops, z < last))
                def _():
                    right(hops, part, z - hops).start()

                @pl.when(jnp.logical_and(z + hops <= last, z > 0))
                def _():
                    left(hops, part, z + hops).start()

        if hops == 0:
            query[...] = jnp.dot(
                wide[...], weight[...], preferred_element_type=jnp.float32
            ).astype(jnp.bfloat16)

    for hops in range(last):
        for part in range(2):

            @pl.when(jnp.logical_and(z >= hops, z < last))
            def _():
                right(hops, part, z - hops).wait_send()

            @pl.when(jnp.logical_and(z + hops <= last, z > 0))
            def _():
                left(hops, part, z + hops).wait_send()

    local.wait()


def ctx_gather(values, wide, weight, ctx_count, fsdp_count, identity):
    rows, columns = values.shape
    vmem = pl.BlockSpec(memory_space=pltpu.VMEM)
    gathered, query = pl.pallas_call(
        functools.partial(ctx_kernel, ctx_count, fsdp_count),
        out_shape=(
            jax.ShapeDtypeStruct((ctx_count, rows, columns), values.dtype),
            jax.ShapeDtypeStruct((rows, weight.shape[1]), values.dtype),
        ),
        in_specs=[pl.BlockSpec(memory_space=pl.ANY), vmem, vmem],
        out_specs=(pl.BlockSpec(memory_space=pl.ANY), vmem),
        scratch_shapes=[
            pltpu.SemaphoreType.DMA((ctx_count, 2)),
            pltpu.SemaphoreType.DMA((ctx_count, 2)),
            pltpu.SemaphoreType.DMA((ctx_count, 2)),
            pltpu.SemaphoreType.DMA((ctx_count, 2)),
            pltpu.SemaphoreType.DMA,
        ],
        compiler_params=pltpu.CompilerParams(
            collective_id=identity, has_side_effects=True, vmem_limit_bytes=VMEM_BYTES
        ),
    )(values, wide, weight)
    return gathered.reshape(ctx_count * rows, columns), query


def scatter_sum(place, partial, pair, stage, inbox, sems):
    pair_send, pair_recv, send, recv = sems
    chips = place.chips

    def swap(step):
        return remote(
            partial.at[place.ahead(step) + 1 - place.core],
            pair.at[step],
            pair_send.at[step],
            pair_recv.at[step],
            (place.z, place.sibling),
        )

    def give(step):
        return remote(
            stage.at[step],
            inbox.at[step],
            send.at[step],
            recv.at[step],
            (place.z, place.ahead(step) + place.core),
        )

    order = list(range(1, chips)) + [0]
    for step in order:
        swap(step).start()
    for step in order:
        swap(step).wait_recv()
        if step > 0:
            both = partial[place.ahead(step) + place.core].astype(jnp.float32) + pair[step].astype(
                jnp.float32
            )
            stage[step] = both.astype(jnp.bfloat16)
            give(step).start()
    result = partial[place.me].astype(jnp.float32) + pair[0].astype(jnp.float32)
    for step in range(1, chips):
        give(step).wait_recv()
        result = result + inbox[step].astype(jnp.float32)
    for step in order:
        swap(step).wait_send()
        if step > 0:
            give(step).wait_send()
    return result


def scatter_scratch(chips, rows, columns):
    return [pltpu.VMEM((chips, rows, columns), jnp.bfloat16) for _ in range(3)] + [
        pltpu.SemaphoreType.DMA((chips,)) for _ in range(4)
    ]


def renoise_kernel(
    ctx_count, fsdp_count, partial, mixed, noise, sig, generated, noisy, out, *scratch
):
    place = Place(ctx_count, fsdp_count)
    greet(place.group_targets())
    gen_sum = scatter_sum(place, partial, *scratch[:3], scratch[3:7])
    value = (mixed[...].astype(jnp.float32) + gen_sum).astype(jnp.bfloat16)
    generated[...] = value
    level = sig[:, :1]
    noisy[...] = (
        (1.0 - level) * value.astype(jnp.float32) + level * noise[...].astype(jnp.float32)
    ).astype(jnp.bfloat16)
    spread = Spread(place, noisy, out, 0, scratch[7:11], 0)
    spread.start()
    local = pltpu.make_async_copy(noisy, out.at[place.me], scratch[11])
    local.start()
    spread.forward()
    spread.corner()
    spread.end()
    local.wait()


def cotangent_kernel(
    ctx_count, fsdp_count, partial, generated, noisy, out, cotangent, *scratch
):
    place = Place(ctx_count, fsdp_count)
    greet(place.group_targets() + place.ctx_targets())
    teacher_sum = scatter_sum(place, partial, *scratch[:3], scratch[3:7])
    real = noisy[...].astype(jnp.float32) + teacher_sum
    cotangent[...] = (generated[...].astype(jnp.float32) - real).astype(jnp.bfloat16)
    ctx_send, ctx_recv, local_sem = scratch[11:14]

    def along(step, source):
        return remote(
            cotangent,
            out.at[source * fsdp_count + place.me],
            ctx_send.at[step],
            ctx_recv.at[step],
            (place.ctx_ahead(step), place.me),
        )

    for step in range(1, ctx_count):
        along(step, place.z).start()
    spreads = [Spread(place, cotangent, out, place.z * fsdp_count, scratch[7:11], 0)]
    spreads[0].start()
    local = pltpu.make_async_copy(cotangent, out.at[place.z * fsdp_count + place.me], local_sem)
    local.start()
    for step in range(1, ctx_count):
        source = place.ctx_behind(step)
        along(step, source).wait_recv()
        row = source * fsdp_count
        spreads.append(
            Spread(place, out.at[row + place.me], out, row, scratch[7:11], step)
        )
        spreads[-1].start()
        spreads[-2].forward()
        if step > 1:
            spreads[-3].corner()
    spreads[-1].forward()
    for spread in spreads[-2:]:
        spread.corner()
    for spread in spreads:
        spread.end()
    for step in range(1, ctx_count):
        along(step, place.z).wait_send()
    local.wait()


def renoise(partial, mixed, noise, sig, ctx_count, fsdp_count, identity):
    rows, columns = mixed.shape
    chips = fsdp_count // 2
    vmem = pl.BlockSpec(memory_space=pltpu.VMEM)
    block = jax.ShapeDtypeStruct((rows, columns), jnp.bfloat16)
    generated, noisy, gathered = pl.pallas_call(
        functools.partial(renoise_kernel, ctx_count, fsdp_count),
        out_shape=(
            block,
            block,
            jax.ShapeDtypeStruct((fsdp_count, rows, columns), jnp.bfloat16),
        ),
        in_specs=[vmem] * 4,
        out_specs=(vmem, vmem, pl.BlockSpec(memory_space=pl.ANY)),
        scratch_shapes=scatter_scratch(chips, rows, columns)
        + spread_sems(1, chips)
        + [pltpu.SemaphoreType.DMA],
        compiler_params=pltpu.CompilerParams(
            collective_id=identity, has_side_effects=True, vmem_limit_bytes=VMEM_BYTES
        ),
    )(
        partial.reshape(fsdp_count, rows, columns),
        mixed,
        noise,
        jnp.broadcast_to(sig, (rows, 128)),
    )
    return generated, noisy, gathered.reshape(fsdp_count * rows, columns)


def all_cotangents(partial, generated, noisy, ctx_count, fsdp_count, identity):
    rows, columns = noisy.shape
    chips = fsdp_count // 2
    vmem = pl.BlockSpec(memory_space=pltpu.VMEM)
    devices = ctx_count * fsdp_count
    gathered = pl.pallas_call(
        functools.partial(cotangent_kernel, ctx_count, fsdp_count),
        out_shape=jax.ShapeDtypeStruct((devices, rows, columns), jnp.bfloat16),
        in_specs=[vmem] * 3,
        out_specs=pl.BlockSpec(memory_space=pl.ANY),
        scratch_shapes=[pltpu.VMEM((rows, columns), jnp.bfloat16)]
        + scatter_scratch(chips, rows, columns)
        + spread_sems(ctx_count, chips)
        + [
            pltpu.SemaphoreType.DMA((ctx_count,)),
            pltpu.SemaphoreType.DMA((ctx_count,)),
            pltpu.SemaphoreType.DMA,
        ],
        compiler_params=pltpu.CompilerParams(
            collective_id=identity, has_side_effects=True, vmem_limit_bytes=VMEM_BYTES
        ),
    )(partial.reshape(fsdp_count, rows, columns), generated, noisy)
    return gathered.reshape(devices * rows, columns)


def per_device(
    clean,
    noise,
    noise_two,
    steps_gen,
    steps_teacher,
    cache_key,
    cache_value,
    cache_block,
    span_block,
    gen_query,
    gen_key,
    gen_value,
    gen_out,
    teacher_query,
    teacher_key,
    teacher_value,
    teacher_out,
):
    ctx_count = lax.axis_size("ctx")
    fsdp_count = lax.axis_size("fsdp")
    tok_dev = clean.shape[0]
    block_rows = tok_dev * fsdp_count
    total = block_rows * ctx_count
    offset = (lax.axis_index("ctx") * fsdp_count + lax.axis_index("fsdp")) * tok_dev
    width = gen_query.shape[1]
    heads = width // HEAD
    sig_gen = sigmas(steps_gen, offset, tok_dev, total)
    mixed = (
        (1.0 - sig_gen) * clean.astype(jnp.float32) + sig_gen * noise.astype(jnp.float32)
    ).astype(jnp.bfloat16)
    slots = cache_block.shape[0]
    visible = (cache_block < span_block[0]).astype(jnp.bfloat16)
    flag_rows = -(-slots // (16 * width)) * 16
    flags = jnp.pad(visible, (0, flag_rows * width - slots)).reshape(flag_rows, width)
    cache = lax.all_gather(
        jnp.concatenate([cache_key, cache_value, flags], axis=0), "ctx", axis=0, tiled=False
    )
    gen_stack = jnp.concatenate([gen_key, gen_value], axis=1)
    wide = normed(group_gather(mixed, ctx_count, fsdp_count, 0))
    projected = jnp.dot(
        wide,
        gen_stack,
        preferred_element_type=jnp.float32,
    ).astype(jnp.bfloat16)
    span, query = ctx_gather(projected, wide, gen_query, ctx_count, fsdp_count, 1)
    query_heads = query.reshape(block_rows, heads, HEAD)
    slots_all = slots * ctx_count
    cached_keys = cache[:, :slots].reshape(slots_all, heads, HEAD)
    cached_values = cache[:, slots : 2 * slots].reshape(slots_all, heads, HEAD)
    allowed = cache[:, 2 * slots :].reshape(ctx_count, -1)[:, :slots].reshape(-1) > 0
    attn = attend(
        query_heads,
        (
            (cached_keys, cached_values, allowed),
            (
                span[:, :width].reshape(total, heads, HEAD),
                span[:, width:].reshape(total, heads, HEAD),
                None,
            ),
        ),
    )
    attn_all = lax.all_gather(attn, "ctx", axis=0, tiled=True)
    sig_teacher = sigmas(steps_teacher, offset, tok_dev, total)
    generated, noisy, noisy_group = renoise(
        jnp.dot(attn, gen_out, preferred_element_type=jnp.float32).astype(jnp.bfloat16),
        mixed,
        noise_two,
        sig_teacher,
        ctx_count,
        fsdp_count,
        2,
    )
    teacher_stack = jnp.concatenate([teacher_key, teacher_value], axis=1)
    t_wide = normed(noisy_group)
    teacher_proj = jnp.dot(
        t_wide,
        teacher_stack,
        preferred_element_type=jnp.float32,
    ).astype(jnp.bfloat16)
    t_span, t_query = ctx_gather(
        teacher_proj, t_wide, teacher_query, ctx_count, fsdp_count, 3
    )
    teacher_heads = t_query.reshape(block_rows, heads, HEAD)
    teacher_attn = attend(
        teacher_heads,
        (
            (
                t_span[:, :width].reshape(total, heads, HEAD),
                t_span[:, width:].reshape(total, heads, HEAD),
                None,
            ),
        ),
    )
    cotangents = all_cotangents(
        jnp.dot(teacher_attn, teacher_out, preferred_element_type=jnp.float32).astype(jnp.bfloat16),
        generated,
        noisy,
        ctx_count,
        fsdp_count,
        4,
    )
    grad_out = lax.dot_general(
        attn_all,
        cotangents,
        (((0,), (0,)), ((), ())),
        preferred_element_type=jnp.float32,
    ).astype(jnp.bfloat16)
    return (generated, grad_out)


def solution(mesh):
    in_specs = (
        P(("ctx", "fsdp"), None),
        P(("ctx", "fsdp"), None),
        P(("ctx", "fsdp"), None),
        P(),
        P(),
        P("ctx", "fsdp"),
        P("ctx", "fsdp"),
        P("ctx"),
        P(),
        P(None, "fsdp"),
        P(None, "fsdp"),
        P(None, "fsdp"),
        P("fsdp", None),
        P(None, "fsdp"),
        P(None, "fsdp"),
        P(None, "fsdp"),
        P("fsdp", None),
    )
    out_specs = (P(("ctx", "fsdp"), None), P("fsdp", None))
    return jax.shard_map(
        per_device, mesh=mesh, in_specs=in_specs, out_specs=out_specs, check_vma=False
    )
```
